32 devices in a mesh: dp: 8 (over y, x, core), seq: 4 (over z).
Axes of the slice: x: 2, y: 2, z: 4, core: 2. Of those that a mesh axis runs over, the one named last changes fastest.
Arguments:
- tokens: bfloat16 [32768, 1024], P(('dp', 'seq')), may hold values from -6 to 6
- norm_gain: float32 [1024], replicated, may hold values from 0.4 to 1.6
- in_proj: bfloat16 [1024, 4384], P('dp'), may hold values from -0.1875 to 0.1875
- conv_weight: float32 [4, 2304], replicated, may hold values from -3 to 3
- conv_bias: float32 [2304], replicated, may hold values from -3 to 3
- dt_bias: float32 [32], replicated, may hold values from -6 to -2
- a_log: float32 [32], replicated, may hold values from -1.5 to 2.5
- skip_d: float32 [32], replicated, may hold values from 0.5 to 1.5
- gate_norm: float32 [2048], replicated, may hold values from 0.4 to 1.6
- out_proj: bfloat16 [2048, 1024], P('dp'), may hold values from -0.125 to 0.125
- cotangent: bfloat16 [32768, 1024], P(('dp', 'seq')), may hold values from -6 to 6
Outputs:
- block_out: bfloat16 [32768, 1024], P(('dp', 'seq'))
- input_grad: bfloat16 [32768, 1024], P(('dp', 'seq'))
- norm_gain_grad: float32 [1024], replicated
- in_proj_grad: float32 [1024, 4384], P('dp', 'seq')
- conv_weight_grad: float32 [4, 2304], replicated
- conv_bias_grad: float32 [2304], replicated
- dt_bias_grad: float32 [32], replicated
- a_log_grad: float32 [32], replicated
- skip_grad: float32 [32], replicated
- gate_norm_grad: float32 [2048], replicated
- out_proj_grad: float32 [2048, 1024], P('dp', 'seq')
The draws below stay inside these ranges and needn't reach their ends.
All inputs are finite; a program needn't handle non-finite values.
Results may differ from the reference program's by a relative error of at most 0.011.
Values may be sent and summed in bfloat16 or wider, within the bound.
A program may use at most 256 MiB of HBM per device.

```python
from functools import partial
import jax
import jax.numpy as jnp
from jax import lax

D = 1024
HEADS = 32
KCONV = 4
BLOCK = 256
DI = 2048
CONVCH = 2304
PROJ = 4384
LENGTH = 4096
SEQS = 8
TOKENS = 32768


def steps_of(rng, extent, shards, least, high):
    level, own = 1.0, jax.random.fold_in(rng, 6)
    for dim, parts in shards:
        draws = jnp.exp(jax.random.uniform(jax.random.fold_in(own, dim), (parts,), jnp.float32, least / len(shards), high / len(shards)))
        level = level * jnp.repeat(draws, extent[dim] // parts).reshape([-1 if axis == dim else 1 for axis in range(len(extent))])
    return level


def bell_draw(rng, dims, width, reach, split=(), kind=jnp.bfloat16):
    entries = width * jax.random.normal(rng, dims, jnp.float32)
    if split:
        entries = entries * steps_of(rng, dims, split, -0.22, 0.18)
    return jnp.clip(entries, -reach, reach).astype(kind)


def setup_inputs(seed: int = 0) -> dict:
    key_list = jax.random.split(jax.random.key(seed), 12)
    tokens = bell_draw(key_list[0], (TOKENS, D), 1.0, 6.0, ((0, 32),))
    norm_gain = jnp.clip(1.0 + 0.12 * jax.random.normal(key_list[1], (D,), jnp.float32), 0.4, 1.6)
    in_proj = bell_draw(key_list[2], (D, PROJ), D ** -0.5, 0.1875, ((0, 8),))
    conv_weight = bell_draw(key_list[3], (KCONV, CONVCH), KCONV ** -0.5, 3.0, (), jnp.float32)
    conv_bias = bell_draw(key_list[4], (CONVCH,), 0.5, 3.0, (), jnp.float32)
    dt_bias = jnp.clip(jax.random.uniform(key_list[5], (HEADS,), jnp.float32, -6.0, -2.0), -6.0, -2.0)
    a_log = jnp.clip(jax.random.uniform(key_list[6], (HEADS,), jnp.float32, -1.5, 2.5), -1.5, 2.5)
    skip_d = jnp.clip(jax.random.uniform(key_list[7], (HEADS,), jnp.float32, 0.5, 1.5), 0.5, 1.5)
    gate_norm = jnp.clip(1.0 + 0.12 * jax.random.normal(key_list[8], (DI,), jnp.float32), 0.4, 1.6)
    out_proj = bell_draw(key_list[9], (DI, D), DI ** -0.5, 0.125, ((0, 8),))
    cotangent = bell_draw(key_list[10], (TOKENS, D), 1.0, 6.0, ((0, 32),))
    return {"tokens": tokens, "norm_gain": norm_gain, "in_proj": in_proj, "conv_weight": conv_weight, "conv_bias": conv_bias, "dt_bias": dt_bias, "a_log": a_log, "skip_d": skip_d, "gate_norm": gate_norm, "out_proj": out_proj, "cotangent": cotangent}


epsilon = 1e-05
highest = lax.Precision.HIGHEST

@jax.custom_vjp
def low(v):
    return lax.optimization_barrier(v.astype(jnp.bfloat16)).astype(jnp.float32)

@jax.custom_vjp
def low_back(v):
    return v

def low_keep(v):
    return (low(v), None)

def low_pass(kept, grad):
    return (grad,)

def back_keep(v):
    return (v, None)

def back_low(kept, grad):
    return (low(grad),)
low.defvjp(low_keep, low_pass)
low_back.defvjp(back_keep, back_low)

def front(inputs, gain_vector):
    return inputs * lax.rsqrt(lax.optimization_barrier(jnp.mean(inputs * inputs, axis=-1, keepdims=True)) + epsilon) * gain_vector

def gated_norm(mixed_values, gate_raw, gain_vector):
    gated_values = mixed_values * jax.nn.silu(gate_raw)
    return gated_values * lax.rsqrt(lax.optimization_barrier(jnp.mean(gated_values * gated_values, axis=-1, keepdims=True)) + epsilon) * gain_vector

def convolve(extended, kernel, offset_bias):
    tap_count = kernel.shape[0]
    rows_out = extended.shape[0] - tap_count + 1
    summed = jnp.broadcast_to(offset_bias[None, :], (rows_out, extended.shape[1]))
    for shift_index in range(tap_count):
        summed = summed + kernel[shift_index][None, :] * extended[shift_index:shift_index + rows_out]
    return jax.nn.silu(summed)

def block_step(carried, pieces, decay_rate, skip_gain):
    block_x, block_dt, block_b, block_c = pieces
    positions = block_dt.shape[0]
    cumulative = jnp.cumsum(block_dt * decay_rate[None, :], axis=0).T
    causal = jnp.arange(positions)[:, None] >= jnp.arange(positions)[None, :]
    spread_gap = cumulative[:, :, None] - cumulative[:, None, :]
    decays = jnp.where(causal[None], jnp.exp(jnp.where(causal[None], spread_gap, 0.0)), 0.0)
    scores = jnp.dot(block_c, block_b.T, precision=highest)
    mixing = scores[None] * decays * block_dt.T[:, None, :]
    heads_x = jnp.transpose(block_x, (1, 0, 2))
    in_block = jnp.einsum('hts,hsp->htp', mixing, heads_x, precision=highest)
    from_state = jnp.einsum('tn,hnp->htp', block_c, carried, precision=highest) * jnp.exp(cumulative)[:, :, None]
    outputs = in_block + from_state + skip_gain[:, None, None] * heads_x
    final_sum = cumulative[:, -1]
    weights_in = jnp.exp(final_sum[:, None] - cumulative) * block_dt.T
    updated = carried * jnp.exp(final_sum)[:, None, None] + jnp.einsum('sn,hsp->hnp', block_b, heads_x * weights_in[:, :, None], precision=highest)
    return (updated, jnp.transpose(outputs, (1, 0, 2)))

def state_space(mixer_x, dt_raw, both_bc, dt_offset, log_rates, skip_gain):
    length_all = mixer_x.shape[0]
    head_count = dt_raw.shape[1]
    head_width = mixer_x.shape[1] // head_count
    state_width = both_bc.shape[1] // 2
    blocks = length_all // BLOCK
    step_dt = jax.nn.softplus(dt_raw + dt_offset[None, :])
    decay_rate = -jnp.exp(log_rates)
    scanned = (mixer_x.reshape(blocks, BLOCK, head_count, head_width), step_dt.reshape(blocks, BLOCK, head_count), both_bc[:, :state_width].reshape(blocks, BLOCK, state_width), both_bc[:, state_width:].reshape(blocks, BLOCK, state_width))
    stepper = jax.checkpoint(partial(block_step, decay_rate=decay_rate, skip_gain=skip_gain))
    initial = jnp.zeros((head_count, state_width, head_width), mixer_x.dtype)
    _, outputs = lax.scan(stepper, initial, scanned)
    return outputs.reshape(length_all, head_count * head_width)

def sequence_forward(inputs, params):
    norm_gain, in_proj, conv_weight, conv_bias, dt_bias, a_log, skip_d, gate_norm, out_proj = params
    inner_width = gate_norm.shape[0]
    channels = conv_bias.shape[0]
    tap_count = conv_weight.shape[0]
    normed = low(front(inputs, norm_gain))
    projected = low(low_back(jnp.dot(normed, in_proj, precision=highest)))
    gate_raw = projected[:, :inner_width]
    conv_in = projected[:, inner_width:inner_width + channels]
    dt_raw = projected[:, inner_width + channels:]
    extended = jnp.concatenate([jnp.zeros((tap_count - 1, channels), conv_in.dtype), conv_in], axis=0)
    activated = convolve(extended, conv_weight, conv_bias)
    mixer_x = low(low_back(activated[:, :inner_width]))
    both_bc = low(activated[:, inner_width:])
    mixed_values = low(low_back(state_space(mixer_x, dt_raw, both_bc, dt_bias, a_log, skip_d)))
    branch_in = low(gated_norm(mixed_values, gate_raw, gate_norm))
    return inputs + jnp.dot(branch_in, out_proj, precision=highest)

def reference(tokens, norm_gain, in_proj, conv_weight, conv_bias, dt_bias, a_log, skip_d, gate_norm, out_proj, cotangent):
    params = (norm_gain.astype(jnp.float32), in_proj.astype(jnp.float32), conv_weight.astype(jnp.float32), conv_bias.astype(jnp.float32), dt_bias.astype(jnp.float32), a_log.astype(jnp.float32), skip_d.astype(jnp.float32), gate_norm.astype(jnp.float32), out_proj.astype(jnp.float32))
    sequences = tokens.astype(jnp.float32).reshape(SEQS, LENGTH, tokens.shape[1])

    def forward(all_inputs, weights_all):

        def one_sequence(carried, inputs):
            return (carried, jax.checkpoint(sequence_forward)(inputs, weights_all))
        _, outputs = lax.scan(one_sequence, jnp.zeros((), jnp.float32), all_inputs)
        return outputs
    outputs, pullback = jax.vjp(forward, sequences, params)
    grad_inputs, grad_params = pullback(cotangent.astype(jnp.float32).reshape(outputs.shape))
    return (outputs.reshape(tokens.shape).astype(jnp.bfloat16), grad_inputs.reshape(tokens.shape).astype(jnp.bfloat16), grad_params[0], grad_params[1], grad_params[2], grad_params[3], grad_params[4], grad_params[5], grad_params[6], grad_params[7], grad_params[8])
```

```python
import jax
import jax.numpy as jnp
from jax import lax
from jax.sharding import PartitionSpec as P

BLOCK = 128


epsilon = 1e-05
highest = lax.Precision.HIGHEST


def passed_along(block, axis, distance):
    devices = range(lax.axis_size(axis))
    route = [(i - distance, i) for i in devices if i - distance in devices]
    return lax.ppermute(block, axis, route)


def front(inputs, gain_vector):
    return (
        inputs
        * lax.rsqrt(jnp.mean(inputs * inputs, axis=-1, keepdims=True) + epsilon)
        * gain_vector
    )


def gated_norm(mixed_values, gate_raw, gain_vector):
    gated_values = mixed_values * jax.nn.silu(gate_raw)
    return (
        gated_values
        * lax.rsqrt(jnp.mean(gated_values * gated_values, axis=-1, keepdims=True) + epsilon)
        * gain_vector
    )


def convolve(extended, kernel, offset_bias):
    tap_count = kernel.shape[0]
    rows_out = extended.shape[0] - tap_count + 1
    summed = jnp.broadcast_to(offset_bias[None, :], (rows_out, extended.shape[1]))
    for shift_index in range(tap_count):
        summed = (
            summed + kernel[shift_index][None, :] * extended[shift_index : shift_index + rows_out]
        )
    return jax.nn.silu(summed)


def chained(finals, decays):
    carried = jnp.zeros_like(finals[0])
    befores = []
    for index in range(finals.shape[0]):
        befores.append(carried)
        carried = carried * decays[index][None, :, None] + finals[index]
    return jnp.stack(befores)


@jax.custom_vjp
def entering_state(final, decay):
    return entering_keep(final, decay)[0]


def entering_keep(final, decay):
    finals = lax.all_gather(final.astype(jnp.bfloat16), "seq").astype(jnp.float32)
    decays = lax.all_gather(decay, "seq")
    befores = chained(finals, decays)
    here = lax.axis_index("seq")
    return lax.dynamic_index_in_dim(befores, here, 0, keepdims=False), (finals, decays)


def entering_back(kept, grad):
    grads = lax.all_gather(grad.astype(jnp.bfloat16), "seq").astype(jnp.float32)
    _, pull = jax.vjp(chained, *kept)
    here = lax.axis_index("seq")
    return tuple(lax.dynamic_index_in_dim(g, here, 0, keepdims=False) for g in pull(grads))


entering_state.defvjp(entering_keep, entering_back)


def state_space(mixer_x, dt_raw, both_bc, dt_offset, log_rates, skip_gain):
    low = jnp.bfloat16
    rows = mixer_x.shape[0]
    heads = dt_raw.shape[1]
    width = mixer_x.shape[1] // heads
    states = both_bc.shape[1] // 2
    blocks = rows // BLOCK
    step_dt = jax.nn.softplus(dt_raw + dt_offset[None, :]).reshape(blocks, BLOCK, heads)
    decay_rate = -jnp.exp(log_rates)
    causal = jnp.arange(BLOCK)[:, None] >= jnp.arange(BLOCK)[None, :]
    cumulative = jnp.einsum(
        "ts,bsh->bht", causal.astype(jnp.float32), step_dt * decay_rate, precision=highest
    )
    steps = jnp.transpose(step_dt, (0, 2, 1))
    block_b = both_bc[:, :states].reshape(blocks, BLOCK, states).astype(low)
    block_c = both_bc[:, states:].reshape(blocks, BLOCK, states).astype(low)
    block_x = mixer_x.reshape(blocks, BLOCK, heads, width)
    spread_gap = cumulative[:, :, :, None] - cumulative[:, :, None, :]
    decays = jnp.where(causal, jnp.exp(jnp.where(causal, spread_gap, 0.0)), 0.0)
    scores = jnp.einsum("btn,bsn->bts", block_c, block_b, preferred_element_type=jnp.float32)
    mixing = scores[:, None] * decays * steps[:, :, None, :]
    in_block = jnp.einsum(
        "bhts,bshp->bthp", mixing.astype(low), block_x.astype(low),
        preferred_element_type=jnp.float32,
    )
    final_sum = cumulative[:, :, -1]
    weights_in = jnp.transpose(jnp.exp(final_sum[:, :, None] - cumulative) * steps, (0, 2, 1))
    weighted = (block_x * weights_in[..., None]).astype(low).reshape(blocks, BLOCK, heads * width)
    added = jnp.einsum("bsn,bsc->bnc", block_b, weighted, preferred_element_type=jnp.float32)
    added = added.reshape(blocks, states, heads, width)
    block_decay = jnp.exp(final_sum)
    local = chained(added, block_decay)
    final = local[-1] * block_decay[-1][None, :, None] + added[-1]
    entered = entering_state(final, jnp.exp(jnp.sum(final_sum, axis=0)))
    reach = jnp.exp(jnp.cumsum(final_sum, axis=0) - final_sum)
    carried = local + reach[:, None, :, None] * entered[None]
    from_state = jnp.einsum(
        "btn,bnc->btc", block_c, carried.astype(low).reshape(blocks, states, heads * width),
        preferred_element_type=jnp.float32,
    ).reshape(blocks, BLOCK, heads, width)
    outputs = (
        in_block
        + from_state * jnp.exp(jnp.transpose(cumulative, (0, 2, 1)))[..., None]
        + skip_gain[:, None] * block_x
    )
    return outputs.reshape(rows, heads * width)


def per_device(
    tokens,
    norm_gain,
    in_proj,
    conv_weight,
    conv_bias,
    dt_bias,
    a_log,
    skip_d,
    gate_norm,
    out_proj,
    cotangent,
):
    inner_width = gate_norm.shape[0]
    channels = conv_bias.shape[0]
    tap_count = conv_weight.shape[0]
    contract_rows = (((0,), (0,)), ((), ()))
    contract_cols = (((1,), (1,)), ((), ()))
    in_rest = lax.all_gather(in_proj[:, inner_width:], "dp", axis=0, tiled=True)
    gate_rows, out_rows, in_rest = lax.optimization_barrier(
        (in_proj[:, :inner_width], out_proj, in_rest)
    )
    in_gate = lax.all_gather(gate_rows, "dp", axis=0, tiled=True)
    out_full = lax.all_gather(out_rows, "dp", axis=0, tiled=True)
    inputs = tokens.astype(jnp.float32)
    normed, front_back = jax.vjp(front, inputs, norm_gain)
    normed_low = normed.astype(jnp.bfloat16)
    projected = jnp.dot(normed_low, in_rest, preferred_element_type=jnp.float32).astype(
        jnp.bfloat16
    )
    conv_in = projected[:, :channels]
    dt_raw = projected[:, channels:]
    rows_here = conv_in.shape[0]
    edge_rows = passed_along(conv_in[rows_here - (tap_count - 1) :], "seq", 1)
    extended = jnp.concatenate([edge_rows, conv_in], axis=0).astype(jnp.float32)
    activated, conv_back = jax.vjp(convolve, extended, conv_weight, conv_bias)
    mixer_x = activated[:, :inner_width].astype(jnp.bfloat16)
    both_bc = activated[:, inner_width:].astype(jnp.bfloat16)
    mixed, mixer_back = jax.vjp(
        state_space,
        mixer_x.astype(jnp.float32),
        dt_raw.astype(jnp.float32),
        both_bc.astype(jnp.float32),
        dt_bias,
        a_log,
        skip_d,
    )
    gate_raw = jnp.dot(normed_low, in_gate, preferred_element_type=jnp.float32).astype(
        jnp.bfloat16
    )
    branch_in, tail_back = jax.vjp(
        gated_norm,
        mixed.astype(jnp.bfloat16).astype(jnp.float32),
        gate_raw.astype(jnp.float32),
        gate_norm,
    )
    branch_low = branch_in.astype(jnp.bfloat16)
    block_out = (inputs + jnp.dot(branch_low, out_full, preferred_element_type=jnp.float32)).astype(
        jnp.bfloat16
    )
    grad_branch = lax.dot_general(
        cotangent, out_full, contract_cols, preferred_element_type=jnp.float32
    )
    grad_mixed, grad_gate_raw, grad_gate_norm = tail_back(grad_branch)
    grad_gate = grad_gate_raw.astype(jnp.bfloat16)
    grad_out_w = lax.dot_general(
        branch_low, cotangent, contract_rows, preferred_element_type=jnp.float32
    ).astype(jnp.bfloat16)
    grad_gate_w = lax.dot_general(
        normed_low, grad_gate, contract_rows, preferred_element_type=jnp.float32
    ).astype(jnp.bfloat16)
    part_out = lax.psum_scatter(grad_out_w, "dp", scatter_dimension=0, tiled=True)
    part_gate = lax.psum_scatter(grad_gate_w, "dp", scatter_dimension=0, tiled=True)
    grad_x, grad_dt, grad_bc, grad_offset, grad_alog, grad_skip = mixer_back(
        grad_mixed.astype(jnp.bfloat16).astype(jnp.float32)
    )
    grad_act = jnp.concatenate(
        [grad_x.astype(jnp.bfloat16).astype(jnp.float32), grad_bc], axis=1
    )
    grad_ext, grad_kernel, grad_cbias = conv_back(grad_act)
    edge_grad = passed_along(grad_ext[: tap_count - 1], "seq", -1)
    grad_conv_in = grad_ext[tap_count - 1 :] + jnp.concatenate(
        [jnp.zeros((rows_here - (tap_count - 1), channels), jnp.float32), edge_grad], axis=0
    )
    grad_rest = jnp.concatenate([grad_conv_in, grad_dt], axis=1).astype(jnp.bfloat16)
    grad_rest_w = lax.dot_general(
        normed_low, grad_rest, contract_rows, preferred_element_type=jnp.float32
    ).astype(jnp.bfloat16)
    grad_rest_w, part_out, part_gate = lax.optimization_barrier((grad_rest_w, part_out, part_gate))
    part_rest = lax.psum_scatter(grad_rest_w, "dp", scatter_dimension=0, tiled=True)
    grad_normed = lax.dot_general(
        grad_gate, in_gate, contract_cols, preferred_element_type=jnp.float32
    ) + lax.dot_general(grad_rest, in_rest, contract_cols, preferred_element_type=jnp.float32)
    grad_inputs, grad_gain = front_back(grad_normed)
    input_grad = (cotangent.astype(jnp.float32) + grad_inputs).astype(jnp.bfloat16)
    part_in = jnp.concatenate([part_gate, part_rest], axis=1).astype(jnp.float32)
    in_proj_grad, out_proj_grad = (
        lax.psum_scatter(part_in, "seq", scatter_dimension=1, tiled=True),
        lax.psum_scatter(part_out.astype(jnp.float32), "seq", scatter_dimension=1, tiled=True),
    )
    smalls = (grad_gain, grad_kernel, grad_cbias, grad_offset, grad_alog, grad_skip, grad_gate_norm)
    joined = lax.psum(jnp.concatenate([v.reshape(-1) for v in smalls]), ("dp", "seq"))
    small_sums, start = [], 0
    for value in smalls:
        small_sums.append(joined[start : start + value.size].reshape(value.shape))
        start += value.size
    return (
        block_out,
        input_grad,
        small_sums[0],
        in_proj_grad,
        *small_sums[1:],
        out_proj_grad,
    )


def solution(mesh):
    in_specs = (
        P(("dp", "seq"), None),
        P(),
        P("dp", None),
        P(),
        P(),
        P(),
        P(),
        P(),
        P(),
        P("dp", None),
        P(("dp", "seq"), None),
    )
    out_specs = (
        P(("dp", "seq"), None),
        P(("dp", "seq"), None),
        P(),
        P("dp", "seq"),
        P(),
        P(),
        P(),
        P(),
        P(),
        P(),
        P("dp", "seq"),
    )
    return jax.shard_map(
        per_device, mesh=mesh, in_specs=in_specs, out_specs=out_specs, check_vma=False
    )
```

```python
import jax
import jax.numpy as jnp
from jax import lax
from jax.experimental import pallas as pl
from jax.experimental.pallas import tpu as pltpu
from jax.sharding import PartitionSpec as P

BLOCK = 128


epsilon = 1e-05
highest = lax.Precision.HIGHEST


def passed_along(block, axis, distance):
    devices = range(lax.axis_size(axis))
    route = [(i - distance, i) for i in devices if i - distance in devices]
    return lax.ppermute(block, axis, route)


def front(inputs, gain_vector):
    return (
        inputs
        * lax.rsqrt(jnp.mean(inputs * inputs, axis=-1, keepdims=True) + epsilon)
        * gain_vector
    )


def gated_norm(mixed_values, gate_raw, gain_vector):
    gated_values = mixed_values * jax.nn.silu(gate_raw)
    return (
        gated_values
        * lax.rsqrt(jnp.mean(gated_values * gated_values, axis=-1, keepdims=True) + epsilon)
        * gain_vector
    )


def convolve(extended, kernel, offset_bias):
    tap_count = kernel.shape[0]
    rows_out = extended.shape[0] - tap_count + 1
    summed = jnp.broadcast_to(offset_bias[None, :], (rows_out, extended.shape[1]))
    for shift_index in range(tap_count):
        summed = (
            summed + kernel[shift_index][None, :] * extended[shift_index : shift_index + rows_out]
        )
    return jax.nn.silu(summed)


LANES = 128
low = jnp.bfloat16
wide = jnp.float32


def dot_nn(a, b):
    return lax.dot_general(a, b, (((1,), (0,)), ((), ())), preferred_element_type=wide)


def dot_nt(a, b):
    return lax.dot_general(a, b, (((1,), (1,)), ((), ())), preferred_element_type=wide)


def dot_tn(a, b):
    return lax.dot_general(a, b, (((0,), (0,)), ((), ())), preferred_element_type=wide)


def pair_columns(values, pair):
    rows = values.shape[0]
    left = lax.broadcasted_iota(jnp.int32, (rows, LANES), 1) < LANES // 2
    return jnp.where(
        left, values[:, 2 * pair : 2 * pair + 1], values[:, 2 * pair + 1 : 2 * pair + 2]
    )


def weighted_kernel(rows_ref, cols_ref, weight_ref, out_ref):
    @pl.when(pl.program_id(0) == 0)
    def _():
        out_ref[...] = jnp.zeros_like(out_ref)

    rows, weights = rows_ref[...], weight_ref[...]
    for pair in range(weights.shape[1] // 2):
        lanes = slice(pair * LANES, (pair + 1) * LANES)
        scaled = (cols_ref[:, lanes].astype(wide) * pair_columns(weights, pair)).astype(low)
        out_ref[:, lanes] += dot_tn(rows, scaled)


def block_decays(cum, cum_t, head, causal):
    gap = cum[:, head : head + 1] - cum_t[head : head + 1, :]
    return jnp.exp(jnp.where(causal, gap, -1e30))


def forward_kernel(
    x_ref, b_ref, c_ref, cum_ref, cum_t_ref, dt_ref, dt_t_ref, skip_ref, enter_ref,
    y_ref, kept_ref, state_ref,
):
    @pl.when(pl.program_id(0) == 0)
    def _():
        state_ref[...] = enter_ref[...]

    block_b, block_c = b_ref[...], c_ref[...]
    cum, cum_t, dt, dt_t = cum_ref[...], cum_t_ref[...], dt_ref[...], dt_t_ref[...]
    scores = dot_nt(block_c, block_b)
    row = lax.broadcasted_iota(jnp.int32, (BLOCK, BLOCK), 0)
    col = lax.broadcasted_iota(jnp.int32, (BLOCK, BLOCK), 1)
    causal = row >= col
    left = lax.broadcasted_iota(jnp.int32, (BLOCK, LANES), 1) < LANES // 2
    for pair in range(dt.shape[1] // 2):
        lanes = slice(pair * LANES, (pair + 1) * LANES)
        x = x_ref[:, lanes]
        x_wide = x.astype(wide)
        state = state_ref[:, lanes]
        state_low = state.astype(low)
        kept_ref[0, :, lanes] = state_low
        cums = pair_columns(cum, pair)
        final = cums[BLOCK - 1 :, :]
        inside = []
        for head in (2 * pair, 2 * pair + 1):
            mixing = scores * block_decays(cum, cum_t, head, causal) * dt_t[head : head + 1, :]
            inside.append(dot_nn(mixing.astype(low), x))
        y = (
            jnp.where(left, inside[0], inside[1])
            + jnp.exp(cums) * dot_nn(block_c, state_low)
            + skip_ref[:, lanes] * x_wide
        )
        y_ref[:, lanes] = y.astype(low)
        weighted = (x_wide * (jnp.exp(final - cums) * pair_columns(dt, pair))).astype(low)
        state_ref[:, lanes] = state * jnp.exp(final) + dot_tn(block_b, weighted)


def backward_kernel(
    x_ref, dy_ref, b_ref, c_ref, cum_ref, cum_t_ref, dt_ref, dt_t_ref, skip_ref, kept_ref,
    leave_ref,
    dx_ref, db_ref, dc_ref, row_ref, weight_ref, col_ref, state_sum_ref, skip_sum_ref, grad_ref,
):
    @pl.when(pl.program_id(0) == 0)
    def _():
        grad_ref[...] = leave_ref[...]

    block_b, block_c = b_ref[...], c_ref[...]
    cum, cum_t, dt, dt_t = cum_ref[...], cum_t_ref[...], dt_ref[...], dt_t_ref[...]
    heads = dt.shape[1]
    scores = dot_nt(block_c, block_b)
    row = lax.broadcasted_iota(jnp.int32, (BLOCK, BLOCK), 0)
    col = lax.broadcasted_iota(jnp.int32, (BLOCK, BLOCK), 1)
    causal = row >= col
    left = lax.broadcasted_iota(jnp.int32, (BLOCK, LANES), 1) < LANES // 2
    slot = lax.broadcasted_iota(jnp.int32, (BLOCK, heads), 1)
    row_sums = jnp.zeros((BLOCK, heads), wide)
    weight_sums = jnp.zeros((BLOCK, heads), wide)
    grad_scores = jnp.zeros((BLOCK, BLOCK), wide)
    grad_b = jnp.zeros((BLOCK, block_b.shape[1]), wide)
    grad_c = jnp.zeros((BLOCK, block_b.shape[1]), wide)
    for pair in range(heads // 2):
        lanes = slice(pair * LANES, (pair + 1) * LANES)
        x, dy = x_ref[:, lanes], dy_ref[:, lanes]
        x_wide, dy_wide = x.astype(wide), dy.astype(wide)
        state_low = kept_ref[0, :, lanes]
        grad = grad_ref[:, lanes]
        grad_low = grad.astype(low)
        cums = pair_columns(cum, pair)
        final = cums[BLOCK - 1 :, :]
        weights = jnp.exp(final - cums) * pair_columns(dt, pair)
        reached = dy_wide * jnp.exp(cums)
        reached_low = reached.astype(low)
        from_state = reached * dot_nn(block_c, state_low)
        to_state = dot_nn(block_b, grad_low)
        weighed = x_wide * to_state
        inside = []
        for side, head in enumerate((2 * pair, 2 * pair + 1)):
            mine = left if side == 0 else jnp.logical_not(left)
            decays = block_decays(cum, cum_t, head, causal)
            steps = dt_t[head : head + 1, :]
            plain = scores * decays
            mixing = (plain * steps).astype(low)
            inside.append(dot_tn(mixing, dy))
            grad_mixing = dot_nt(jnp.where(mine, dy, jnp.zeros_like(dy)), x)
            grad_plain = grad_mixing * plain
            grad_scores = grad_scores + grad_mixing * decays * steps
            sums = grad_plain * steps + jnp.where(mine, from_state, 0.0)
            row_sums = jnp.where(slot == head, jnp.sum(sums, axis=1, keepdims=True), row_sums)
            weight_sums = jnp.where(
                slot == head,
                jnp.sum(jnp.where(mine, weighed, 0.0), axis=1, keepdims=True),
                weight_sums,
            )
            col_ref[head : head + 1, :] = jnp.sum(grad_plain, axis=0, keepdims=True)
        dx_ref[:, lanes] = (
            jnp.where(left, inside[0], inside[1])
            + weights * to_state
            + skip_ref[:, lanes] * dy_wide
        ).astype(low)
        grad_c = grad_c + dot_nt(reached_low, state_low)
        grad_b = grad_b + dot_nt((x_wide * weights).astype(low), grad_low)
        state_sum_ref[0, :, lanes] = jnp.sum(
            grad * state_low.astype(wide), axis=0, keepdims=True
        )
        skip_sum_ref[0, :, lanes] = jnp.sum(dy_wide * x_wide, axis=0, keepdims=True)
        grad_ref[:, lanes] = grad * jnp.exp(final) + dot_tn(block_c, reached_low)
    scores_low = grad_scores.astype(low)
    dc_ref[...] = grad_c + dot_nn(scores_low, block_b)
    db_ref[...] = grad_b + dot_tn(scores_low, block_c)
    row_ref[...] = row_sums
    weight_ref[...] = weight_sums


def sequential():
    return pltpu.CompilerParams(
        dimension_semantics=("arbitrary",), vmem_limit_bytes=40 * 1024 * 1024
    )


def weighted_total(rows, cols, weights):
    length, states = rows.shape
    inner, heads = cols.shape[1], weights.shape[1]
    return pl.pallas_call(
        weighted_kernel,
        grid=(length // BLOCK,),
        in_specs=[
            pl.BlockSpec((BLOCK, states), lambda i: (i, 0)),
            pl.BlockSpec((BLOCK, inner), lambda i: (i, 0)),
            pl.BlockSpec((BLOCK, heads), lambda i: (i, 0)),
        ],
        out_specs=pl.BlockSpec((states, inner), lambda i: (0, 0)),
        out_shape=jax.ShapeDtypeStruct((states, inner), wide),
        compiler_params=sequential(),
        cost_estimate=pl.CostEstimate(
            flops=2 * length * states * inner, bytes_accessed=6 * length * inner, transcendentals=0
        ),
    )(rows, cols, weights)


def scan_specs(states, inner, heads, place):
    return dict(
        wide_rows=pl.BlockSpec((BLOCK, inner), lambda i: (place(i), 0)),
        state_rows=pl.BlockSpec((BLOCK, states), lambda i: (place(i), 0)),
        head_rows=pl.BlockSpec((BLOCK, heads), lambda i: (place(i), 0)),
        head_cols=pl.BlockSpec((heads, BLOCK), lambda i: (0, place(i))),
        skip=pl.BlockSpec((1, inner), lambda i: (0, 0)),
        state=pl.BlockSpec((states, inner), lambda i: (0, 0)),
        kept=pl.BlockSpec((1, states, inner), lambda i: (place(i), 0, 0)),
        sums=pl.BlockSpec((1, 1, inner), lambda i: (place(i), 0, 0)),
    )


def scan_forward(x, b, c, cum, cum_t, dt, dt_t, skip, enter):
    length, inner = x.shape
    states, heads = b.shape[1], dt.shape[1]
    blocks = length // BLOCK
    p = scan_specs(states, inner, heads, lambda i: i)
    return pl.pallas_call(
        forward_kernel,
        grid=(blocks,),
        in_specs=[
            p["wide_rows"], p["state_rows"], p["state_rows"], p["head_rows"], p["head_cols"],
            p["head_rows"], p["head_cols"], p["skip"], p["state"],
        ],
        out_specs=[p["wide_rows"], p["kept"]],
        out_shape=[
            jax.ShapeDtypeStruct((length, inner), low),
            jax.ShapeDtypeStruct((blocks, states, inner), low),
        ],
        scratch_shapes=[pltpu.VMEM((states, inner), wide)],
        compiler_params=sequential(),
        cost_estimate=pl.CostEstimate(
            flops=10 * length * states * inner, bytes_accessed=8 * length * inner,
            transcendentals=length * BLOCK * heads,
        ),
    )(x, b, c, cum, cum_t, dt, dt_t, skip, enter)


def scan_backward(x, dy, b, c, cum, cum_t, dt, dt_t, skip, kept, leave):
    length, inner = x.shape
    states, heads = b.shape[1], dt.shape[1]
    blocks = length // BLOCK
    p = scan_specs(states, inner, heads, lambda i: blocks - 1 - i)
    return pl.pallas_call(
        backward_kernel,
        grid=(blocks,),
        in_specs=[
            p["wide_rows"], p["wide_rows"], p["state_rows"], p["state_rows"], p["head_rows"],
            p["head_cols"], p["head_rows"], p["head_cols"], p["skip"], p["kept"], p["state"],
        ],
        out_specs=[
            p["wide_rows"], p["state_rows"], p["state_rows"], p["head_rows"], p["head_rows"],
            p["head_cols"], p["sums"], p["sums"],
        ],
        out_shape=[
            jax.ShapeDtypeStruct((length, inner), low),
            jax.ShapeDtypeStruct((length, states), wide),
            jax.ShapeDtypeStruct((length, states), wide),
            jax.ShapeDtypeStruct((length, heads), wide),
            jax.ShapeDtypeStruct((length, heads), wide),
            jax.ShapeDtypeStruct((heads, length), wide),
            jax.ShapeDtypeStruct((blocks, 1, inner), wide),
            jax.ShapeDtypeStruct((blocks, 1, inner), wide),
        ],
        scratch_shapes=[pltpu.VMEM((states, inner), wide)],
        compiler_params=sequential(),
        cost_estimate=pl.CostEstimate(
            flops=24 * length * states * inner, bytes_accessed=12 * length * inner,
            transcendentals=length * BLOCK * heads,
        ),
    )(x, dy, b, c, cum, cum_t, dt, dt_t, skip, kept, leave)


def state_space(x, dt_raw, b, c, dt_offset, log_rates, skip_gain):
    length, inner = x.shape
    heads, states = dt_raw.shape[1], b.shape[1]
    head_width = inner // heads
    blocks = length // BLOCK
    shifted = dt_raw.astype(wide) + dt_offset[None, :]
    dt = jax.nn.softplus(shifted)
    rate = -jnp.exp(log_rates)
    lower = (jnp.arange(BLOCK)[:, None] >= jnp.arange(BLOCK)[None, :]).astype(wide)
    cum_blocks = jnp.einsum(
        "ts,bsh->bth", lower, (dt * rate).reshape(blocks, BLOCK, heads), precision=highest
    )
    cum = cum_blocks.reshape(length, heads)
    final = cum_blocks[:, -1]
    reach = jnp.cumsum(final, axis=0)
    since = (cum_blocks + (reach - final)[:, None]).reshape(length, heads)
    total = reach[-1]
    added = weighted_total(b, x, jnp.exp(total[None] - since) * dt)
    decay = jnp.repeat(jnp.exp(total), head_width)[None]
    coarse = decay.astype(low)
    fine = (decay - coarse.astype(wide)).astype(low)
    sent = jnp.concatenate(
        [added.astype(low), coarse, fine, jnp.zeros((14, inner), low)], axis=0
    )
    everyone = lax.all_gather(sent, "seq")
    here, count = lax.axis_index("seq"), lax.axis_size("seq")
    decays = everyone[:, states].astype(wide) + everyone[:, states + 1].astype(wide)
    enter = jnp.zeros((states, inner), wide)
    for index in range(count - 1):
        moved = enter * decays[index][None] + everyone[index, :states].astype(wide)
        enter = jnp.where(index < here, moved, enter)
    cum_t, dt_t = cum.T, dt.T
    skip = jnp.repeat(skip_gain, head_width)[None]
    y, kept = scan_forward(x, b, c, cum, cum_t, dt, dt_t, skip, enter)

    def pull(dy):
        leaving = lax.all_gather(weighted_total(c, dy, jnp.exp(since)).astype(low), "seq")
        leave = jnp.zeros((states, inner), wide)
        for index in range(count - 1, 0, -1):
            moved = leave * decays[index][None] + leaving[index].astype(wide)
            leave = jnp.where(index > here, moved, leave)
        dx, db, dc, row_sums, weight_sums, col_sums, state_sums, skip_sums = scan_backward(
            x, dy, b, c, cum, cum_t, dt, dt_t, skip, kept, leave
        )
        columns = col_sums.T
        ended = jnp.exp(final[:, None] - cum_blocks).reshape(length, heads)
        through = weight_sums * ended * dt
        grad_cum = (row_sums - dt * columns - through).reshape(blocks, BLOCK, heads)
        kept_sums = jnp.sum(state_sums.reshape(blocks, heads, head_width), axis=2)
        grad_final = (
            jnp.sum(through.reshape(blocks, BLOCK, heads), axis=1) + jnp.exp(final) * kept_sums
        )
        grad_step = (
            jnp.einsum("ts,bth->bsh", lower, grad_cum, precision=highest) + grad_final[:, None]
        ).reshape(length, heads)
        grad_dt = columns + weight_sums * ended + grad_step * rate
        grad_raw = grad_dt * jax.nn.sigmoid(shifted)
        grad_skip = jnp.sum(skip_sums.reshape(blocks, heads, head_width), axis=(0, 2))
        return (
            dx, grad_raw, db, dc, jnp.sum(grad_raw, axis=0),
            rate * jnp.sum(grad_step * dt, axis=0), grad_skip,
        )

    return y, pull


def per_device(
    tokens,
    norm_gain,
    in_proj,
    conv_weight,
    conv_bias,
    dt_bias,
    a_log,
    skip_d,
    gate_norm,
    out_proj,
    cotangent,
):
    inner_width = gate_norm.shape[0]
    channels = conv_bias.shape[0]
    tap_count = conv_weight.shape[0]
    contract_rows = (((0,), (0,)), ((), ()))
    contract_cols = (((1,), (1,)), ((), ()))
    in_rest = lax.all_gather(in_proj[:, inner_width:], "dp", axis=0, tiled=True)
    gate_rows, out_rows, in_rest = lax.optimization_barrier(
        (in_proj[:, :inner_width], out_proj, in_rest)
    )
    in_gate = lax.all_gather(gate_rows, "dp", axis=0, tiled=True)
    out_full = lax.all_gather(out_rows, "dp", axis=0, tiled=True)
    inputs = tokens.astype(jnp.float32)
    normed, front_back = jax.vjp(front, inputs, norm_gain)
    normed_low = normed.astype(jnp.bfloat16)
    projected = jnp.dot(normed_low, in_rest, preferred_element_type=jnp.float32).astype(
        jnp.bfloat16
    )
    conv_in = projected[:, :channels]
    dt_raw = projected[:, channels:]
    rows_here = conv_in.shape[0]
    edge_rows = passed_along(conv_in[rows_here - (tap_count - 1) :], "seq", 1)
    extended = jnp.concatenate([edge_rows, conv_in], axis=0).astype(jnp.float32)
    activated, conv_back = jax.vjp(convolve, extended, conv_weight, conv_bias)
    states = (channels - inner_width) // 2
    activated = activated.astype(low)
    mixed, mixer_back = state_space(
        activated[:, :inner_width],
        dt_raw,
        activated[:, inner_width : inner_width + states],
        activated[:, inner_width + states :],
        dt_bias,
        a_log,
        skip_d,
    )
    gate_raw = jnp.dot(normed_low, in_gate, preferred_element_type=jnp.float32).astype(
        jnp.bfloat16
    )
    branch_in, tail_back = jax.vjp(
        gated_norm,
        mixed.astype(jnp.float32),
        gate_raw.astype(jnp.float32),
        gate_norm,
    )
    branch_low = branch_in.astype(jnp.bfloat16)
    block_out = (inputs + jnp.dot(branch_low, out_full, preferred_element_type=jnp.float32)).astype(
        jnp.bfloat16
    )
    grad_branch = lax.dot_general(
        cotangent, out_full, contract_cols, preferred_element_type=jnp.float32
    )
    grad_mixed, grad_gate_raw, grad_gate_norm = tail_back(grad_branch)
    grad_gate = grad_gate_raw.astype(jnp.bfloat16)
    grad_out_w = lax.dot_general(
        branch_low, cotangent, contract_rows, preferred_element_type=jnp.float32
    ).astype(jnp.bfloat16)
    grad_gate_w = lax.dot_general(
        normed_low, grad_gate, contract_rows, preferred_element_type=jnp.float32
    ).astype(jnp.bfloat16)
    part_out = lax.psum_scatter(grad_out_w, "dp", scatter_dimension=0, tiled=True)
    part_gate = lax.psum_scatter(grad_gate_w, "dp", scatter_dimension=0, tiled=True)
    grad_x, grad_dt, grad_b, grad_c, grad_offset, grad_alog, grad_skip = mixer_back(
        grad_mixed.astype(low)
    )
    grad_act = jnp.concatenate([grad_x.astype(wide), grad_b, grad_c], axis=1)
    grad_ext, grad_kernel, grad_cbias = conv_back(grad_act)
    edge_grad = passed_along(grad_ext[: tap_count - 1], "seq", -1)
    grad_conv_in = grad_ext[tap_count - 1 :] + jnp.concatenate(
        [jnp.zeros((rows_here - (tap_count - 1), channels), jnp.float32), edge_grad], axis=0
    )
    grad_rest = jnp.concatenate([grad_conv_in, grad_dt], axis=1).astype(jnp.bfloat16)
    grad_rest_w = lax.dot_general(
        normed_low, grad_rest, contract_rows, preferred_element_type=jnp.float32
    ).astype(jnp.bfloat16)
    grad_rest_w, part_out, part_gate = lax.optimization_barrier((grad_rest_w, part_out, part_gate))
    part_rest = lax.psum_scatter(grad_rest_w, "dp", scatter_dimension=0, tiled=True)
    grad_normed = lax.dot_general(
        grad_gate, in_gate, contract_cols, preferred_element_type=jnp.float32
    ) + lax.dot_general(grad_rest, in_rest, contract_cols, preferred_element_type=jnp.float32)
    grad_inputs, grad_gain = front_back(grad_normed)
    input_grad = (cotangent.astype(jnp.float32) + grad_inputs).astype(jnp.bfloat16)
    part_in = jnp.concatenate([part_gate, part_rest], axis=1).astype(jnp.float32)
    in_proj_grad, out_proj_grad = (
        lax.psum_scatter(part_in, "seq", scatter_dimension=1, tiled=True),
        lax.psum_scatter(part_out.astype(jnp.float32), "seq", scatter_dimension=1, tiled=True),
    )
    smalls = (grad_gain, grad_kernel, grad_cbias, grad_offset, grad_alog, grad_skip, grad_gate_norm)
    joined = jnp.concatenate([v.reshape(-1) for v in smalls])
    joined = jnp.pad(joined, (0, -joined.size % (8 * LANES))).reshape(-1, LANES)
    rows_sent = joined.shape[0]
    joined = lax.all_gather(joined, ("dp", "seq"), axis=0, tiled=True)
    joined = jnp.sum(joined.reshape(-1, rows_sent, LANES), axis=0).reshape(-1)
    small_sums, start = [], 0
    for value in smalls:
        small_sums.append(joined[start : start + value.size].reshape(value.shape))
        start += value.size
    return (
        block_out,
        input_grad,
        small_sums[0],
        in_proj_grad,
        *small_sums[1:],
        out_proj_grad,
    )


def solution(mesh):
    in_specs = (
        P(("dp", "seq"), None),
        P(),
        P("dp", None),
        P(),
        P(),
        P(),
        P(),
        P(),
        P(),
        P("dp", None),
        P(("dp", "seq"), None),
    )
    out_specs = (
        P(("dp", "seq"), None),
        P(("dp", "seq"), None),
        P(),
        P("dp", "seq"),
        P(),
        P(),
        P(),
        P(),
        P(),
        P(),
        P("dp", "seq"),
    )
    return jax.shard_map(
        per_device, mesh=mesh, in_specs=in_specs, out_specs=out_specs, check_vma=False
    )
```
